32 devices in a mesh: row: 4 (over y, x), col: 8 (over z, core).
Axes of the slice: x: 2, y: 2, z: 4, core: 2. Of those that a mesh axis runs over, the one named last changes fastest.
Arguments:
- amplitudes: bfloat16 [24576, 24576], P('row', 'col'), may hold values from -4 to 4
- cholesky: bfloat16 [24576, 512], P('row'), may hold values from -6 to 6
- gaps: float32 [24576], replicated, may hold values from 0.5 to 2
Outputs:
- final_amplitudes: bfloat16 [24576, 24576], P('row', 'col')
The draws below stay inside these ranges and needn't reach their ends.
All inputs are finite; a program needn't handle non-finite values.
Results may differ from the reference program's by a relative error of at most 0.0057.
Values may be sent and summed in bfloat16 or wider, within the bound.
No kernel may reach another device: no remote copies, remote signals or barrier semaphores. Data moves between devices by JAX's collectives and lax.ppermute only.
A program may use at most 128 MiB of HBM per device.

```python
import math
import jax
import jax.numpy as jnp
from jax import lax

P_SIZE = 24576
L = 512
ITERS = 1
N_ROW = 4


def raised(values, stream_key, source, target, blocks, factor):
    owner, partner = [(jnp.arange(values.shape[position]) // (values.shape[position] // blocks)).reshape([-1 if axis == position else 1 for axis in range(values.ndim)]) for position in (source, target)]
    chosen = jax.random.permutation(stream_key, blocks)[partner]
    strong = (owner == chosen) | (owner == (partner + blocks // 2) % blocks)
    return jnp.where(strong, factor * values, values)


def block_levels(key, shape, cuts, least, top_value):
    gain = 1.0
    for position, parts in cuts:
        heights = jax.random.uniform(jax.random.fold_in(jax.random.fold_in(key, 6), position), (parts,), jnp.float32, least / len(cuts), top_value / len(cuts))
        gain = gain * jnp.repeat(jnp.exp(heights), shape[position] // parts).reshape((-1,) + (1,) * (len(shape) - 1 - position))
    return gain


def centred(rng, shape, spread, most, cuts=(), kind=jnp.bfloat16):
    result = spread * jax.random.normal(rng, shape, jnp.float32)
    if cuts:
        result = result * block_levels(rng, shape, cuts, -0.22, 0.18)
    return jnp.clip(result, -most, most).astype(kind)


def gaussian_with(key, shape, deviation, bound, cuts, heavy, dtype=jnp.bfloat16):
    drawn = deviation * jax.random.normal(key, shape, jnp.float32)
    if cuts:
        drawn = drawn * block_levels(key, shape, cuts, -0.22, 0.18)
    return jnp.clip(raised(drawn, jax.random.fold_in(key, 3), *heavy), -bound, bound).astype(dtype)


def setup_inputs(seed: int = 0) -> dict:
    splits = jax.random.split(jax.random.key(seed), 4)
    amplitudes = gaussian_with(splits[0], (P_SIZE, P_SIZE), 0.5, 4.0, ((0, 4), (1, 8)), (1, 0, 8, 2.0))
    cholesky = centred(splits[1], (P_SIZE, L), 1.0, 6.0, ((0, 4),))
    gaps = jnp.clip(jnp.exp(jax.random.uniform(splits[2], (P_SIZE,), jnp.float32, math.log(0.5), math.log(2.0))), 0.5, 2.0)
    return dict(amplitudes=amplitudes, cholesky=cholesky, gaps=gaps)


def dress(current, cholesky):
    product = jnp.dot(current, cholesky, preferred_element_type=jnp.float32)
    return (cholesky.astype(jnp.float32) + product * (P_SIZE ** -0.5)).astype(jnp.bfloat16)


def contract(dressed, gaps):
    block_rows = P_SIZE // N_ROW
    blocks = dressed.reshape(N_ROW, block_rows, L)
    gap_blocks = gaps.reshape(N_ROW, block_rows)

    def one_block(pair):
        rows_part, gap_part = pair
        product = jnp.dot(rows_part, dressed.T, preferred_element_type=jnp.float32)
        return (-(product * (L ** -0.5)) / (gap_part[:, None] + gaps[None, :])).astype(jnp.bfloat16)

    return lax.map(one_block, (blocks, gap_blocks)).reshape(P_SIZE, P_SIZE)


def reference(amplitudes, cholesky, gaps):
    current = amplitudes
    for iteration in range(ITERS):
        dressed = dress(current, cholesky)
        current = contract(dressed, gaps)
    return current
```

```python
import functools

import jax
import jax.numpy as jnp
from jax import lax
from jax.experimental import pallas as pl
from jax.experimental.pallas import tpu as pltpu
from jax.sharding import PartitionSpec as P

BF16, F32 = jnp.bfloat16, jnp.float32
VMEM_LIMIT = 56 * 1024 * 1024
SHARES = (1, 2, 1)


def spread(value, axis, source):
    kept = jnp.where(lax.axis_index(axis) == source, value, 0).astype(value.dtype)
    return lax.psum(kept, axis)


def general_shards(amplitudes, cholesky, gaps):
    rows_dev, cols_dev = amplitudes.shape
    pairs, vectors = gaps.shape[0], cholesky.shape[1]
    first_col = lax.axis_index("col") * cols_dev
    root_row = first_col // rows_dev
    offset = first_col - root_row * rows_dev
    chol_cols = spread(
        lax.dynamic_slice_in_dim(cholesky, offset, cols_dev, 0), "row", root_row
    )
    gap_rows = lax.dynamic_slice_in_dim(
        gaps, lax.axis_index("row") * rows_dev, rows_dev, 0
    )
    gap_cols = lax.dynamic_slice_in_dim(gaps, first_col, cols_dev, 0)
    pieces = rows_dev // lax.axis_size("col")
    own_rows = lax.dynamic_slice_in_dim(
        cholesky, lax.axis_index("col") * pieces, pieces, 0
    ).astype(F32)
    summed = lax.psum_scatter(
        jnp.dot(amplitudes, chol_cols, preferred_element_type=F32),
        "col",
        scatter_dimension=0,
        tiled=True,
    )
    dressed = (own_rows + summed * pairs**-0.5).astype(BF16)
    w_rows = lax.all_gather(dressed, "col", axis=0, tiled=True)
    w_cols = spread(
        lax.dynamic_slice_in_dim(w_rows, offset, cols_dev, 0), "row", root_row
    )
    product = lax.dot_general(
        w_rows, w_cols, (((1,), (1,)), ((), ())), preferred_element_type=F32
    )
    return (
        -(product * vectors**-0.5) / (gap_rows[:, None] + gap_cols[None, :])
    ).astype(BF16)


def params():
    return pltpu.CompilerParams(vmem_limit_bytes=VMEM_LIMIT)


def cost(flops, nbytes):
    return pl.CostEstimate(flops=flops, bytes_accessed=nbytes, transcendentals=0)


def partial_kernel(k_ref, a0_ref, a1_ref, c_ref, *refs):
    own_ref, oth_ref = refs[-2:]
    own_ref[...] = jnp.dot(a0_ref[...], c_ref[...], preferred_element_type=F32)
    oth_ref[...] = jnp.dot(
        a1_ref[...], c_ref[...], preferred_element_type=F32
    ).astype(BF16)


def partial_sums(core, tile, vectors, after):
    rows = tile.shape[0]
    depth, width = vectors.shape
    half = rows // 2
    step = min(256, half)
    per_half = half // step
    return pl.pallas_call(
        partial_kernel,
        grid_spec=pltpu.PrefetchScalarGridSpec(
            num_scalar_prefetch=1,
            grid=(per_half,),
            in_specs=[
                pl.BlockSpec((step, depth), lambda i, k: (k[0] * per_half + i, 0)),
                pl.BlockSpec((step, depth), lambda i, k: ((1 - k[0]) * per_half + i, 0)),
                pl.BlockSpec((depth, width), lambda i, k: (0, 0)),
            ]
            + [pl.BlockSpec(memory_space=pl.ANY)] * len(after),
            out_specs=[
                pl.BlockSpec((step, width), lambda i, k: (i, 0)),
                pl.BlockSpec((step, width), lambda i, k: (i, 0)),
            ],
        ),
        out_shape=[
            jax.ShapeDtypeStruct((half, width), F32),
            jax.ShapeDtypeStruct((half, width), BF16),
        ],
        compiler_params=params(),
        cost_estimate=cost(2 * rows * depth * max(width, 256), 2 * rows * depth + 3 * rows * width),
        name="partial_sums",
    )(core, tile, tile, vectors, *after)


def final_kernel(shares, k_ref, *refs):
    own, oth, cols = refs[:shares], refs[shares : 2 * shares], refs[2 * shares : 3 * shares]
    gr_ref, gc_ref, out_ref, w_cols, w_rows = refs[3 * shares :]
    step = pl.program_id(0)

    @pl.when(step == 0)
    def _():
        first = 0
        for c_ref in cols:
            w_cols[:, first : first + c_ref.shape[1]] = c_ref[...]
            first += c_ref.shape[1]

    mine = (2 * step) // pl.num_programs(0) == k_ref[0]
    first = 0
    for own_ref, oth_ref in zip(own, oth):
        w_rows[:, first : first + own_ref.shape[1]] = jnp.where(mine, own_ref[...], oth_ref[...])
        first += own_ref.shape[1]
    piece = min(768, w_cols.shape[0])
    for first in range(0, w_cols.shape[0], piece):
        here = slice(first, first + piece)
        product = lax.dot_general(
            w_rows[...], w_cols[here, :], (((1,), (1,)), ((), ())), preferred_element_type=F32
        )
        wide = jnp.concatenate([gr_ref[...]] * (piece // gr_ref.shape[1]), axis=1)
        out_ref[:, here] = (product / (wide + gc_ref[:, here])).astype(BF16)


def final_product(core, own, oth, cols, gap_rows, gap_cols):
    shares = len(own)
    half, width = own[0].shape[0], cols[0].shape[0]
    vectors = sum(c.shape[1] for c in cols)
    step = min(768, half)
    per_half = half // step
    return pl.pallas_call(
        functools.partial(final_kernel, shares),
        grid_spec=pltpu.PrefetchScalarGridSpec(
            num_scalar_prefetch=1,
            grid=(2 * per_half,),
            in_specs=[
                pl.BlockSpec((step, w.shape[1]), lambda i, k: (lax.rem(i, per_half), 0))
                for w in (*own, *oth)
            ]
            + [pl.BlockSpec(c.shape, lambda i, k: (0, 0)) for c in cols]
            + [
                pl.BlockSpec((step, gap_rows.shape[1]), lambda i, k: (i, 0)),
                pl.BlockSpec((1, width), lambda i, k: (0, 0)),
            ],
            out_specs=pl.BlockSpec((step, width), lambda i, k: (i, 0)),
            scratch_shapes=[
                pltpu.VMEM((width, vectors), BF16),
                pltpu.VMEM((step, vectors), BF16),
            ],
        ),
        out_shape=jax.ShapeDtypeStruct((2 * half, width), BF16),
        compiler_params=params(),
        cost_estimate=cost(4 * half * width * vectors, 4 * half * width),
        name="final_product",
    )(core, *own, *oth, *cols, gap_rows, gap_cols)


def planned_shards(amplitudes, cholesky, gaps):
    rows_dev, cols_dev = amplitudes.shape
    pairs, vectors = gaps.shape[0], cholesky.shape[1]
    n_col = lax.axis_size("col")
    planes = n_col // 2
    row, col = lax.axis_index("row"), lax.axis_index("col")
    plane, core = col // 2, col % 2
    core_arg = core.astype(jnp.int32).reshape(1)
    half = rows_dev // 2
    groups = [[2 * plane_ + core_ for plane_ in range(planes)] for core_ in range(2)]

    def in_plane(*hops):
        pairs_list = [
            ((plane_ ^ source) * n_col + 2 * plane_ + core_, (plane_ ^ target) * n_col + 2 * plane_ + core_)
            for source, target in hops
            for plane_ in range(planes)
            for core_ in range(2)
        ]
        return lambda value: lax.ppermute(value, ("row", "col"), pairs_list)

    root_x, root_y = in_plane((0, 1)), in_plane((0, 2))
    x_far, y_far = in_plane((1, 3)), in_plane((2, 3))
    swap = lambda value: lax.ppermute(value, "col", [(i, i ^ 1) for i in range(n_col)])
    is_root = row == plane

    def tied(value, others):
        return lax.optimization_barrier((value, *others))[0]

    def to_plane(low, high):
        low_x, high_y = root_x(low), root_y(high)
        low_far, high_far = x_far(low_x), y_far(high_y)
        high_x, low_y = root_x(high), root_y(low)
        everywhere = jnp.concatenate(
            [
                jnp.where(is_root, low, low_x + low_y + low_far),
                jnp.where(is_root, high, high_x + high_y + high_far),
            ],
            axis=0,
        )
        return everywhere, (low_x, high_y), (high_x, low_y)

    scale = pairs**-0.5
    gap_scale = -(vectors**0.5)
    gap_rows = lax.dynamic_slice_in_dim(gaps, row * rows_dev, rows_dev, 0) * gap_scale
    gap_rows = jnp.broadcast_to(gap_rows[:, None], (rows_dev, 128))
    gap_cols = (lax.dynamic_slice_in_dim(gaps, col * cols_dev, cols_dev, 0) * gap_scale)[None, :]

    first = 0
    own, oth, cols = [], [], []
    sent = after = hops = ()
    for share in SHARES:
        width = vectors * share // sum(SHARES)
        low = lax.dynamic_slice(cholesky, (core * half, first), (half // 2, width))
        high = lax.dynamic_slice(cholesky, (core * half + half // 2, first), (half // 2, width))
        chol_cols, _, sent = to_plane(tied(low, sent), tied(high, sent))
        mine, other = partial_sums(core_arg, amplitudes, chol_cols, after)
        pair = (mine + swap(other).astype(F32)).astype(BF16)
        summed = lax.psum_scatter(
            pair, "col", scatter_dimension=0, tiled=True, axis_index_groups=groups
        )
        piece = summed.shape[0]
        chol = lax.dynamic_slice(cholesky, (core * half + plane * piece, first), (piece, width))
        dressed = (chol.astype(F32) + tied(summed, hops).astype(F32) * scale).astype(BF16)
        w_own = lax.all_gather(dressed, "col", axis=0, tiled=True, axis_index_groups=groups)
        own.append(w_own)
        oth.append(swap(w_own))
        everywhere, early, _ = to_plane(w_own[: half // 2], w_own[half // 2 :])
        cols.append(everywhere)
        after = (pair,) if len(own) == 1 else (dressed,)
        hops = (everywhere,) if len(own) == 1 else early
        first += width
    return final_product(core_arg, own, oth, cols, gap_rows, gap_cols)


def solution(mesh):
    in_specs = (P("row", "col"), P("row", None), P())
    out_specs = P("row", "col")
    fits = (mesh.shape["row"], mesh.shape["col"]) == (4, 8)
    shards = planned_shards if fits else general_shards
    return jax.shard_map(
        shards, mesh=mesh, in_specs=in_specs, out_specs=out_specs, check_vma=False
    )
```

```python
import functools

import jax
import jax.numpy as jnp
from jax import lax
from jax.experimental import pallas as pl
from jax.experimental.pallas import tpu as pltpu
from jax.sharding import PartitionSpec as P

BF16, F32 = jnp.bfloat16, jnp.float32
VMEM_LIMIT = 56 * 1024 * 1024
CHUNKS = 4


def spread(value, axis, source):
    kept = jnp.where(lax.axis_index(axis) == source, value, 0).astype(value.dtype)
    return lax.psum(kept, axis)


def general_shards(amplitudes, cholesky, gaps):
    rows_dev, cols_dev = amplitudes.shape
    pairs, vectors = gaps.shape[0], cholesky.shape[1]
    first_col = lax.axis_index("col") * cols_dev
    root_row = first_col // rows_dev
    offset = first_col - root_row * rows_dev
    chol_cols = spread(
        lax.dynamic_slice_in_dim(cholesky, offset, cols_dev, 0), "row", root_row
    )
    gap_rows = lax.dynamic_slice_in_dim(
        gaps, lax.axis_index("row") * rows_dev, rows_dev, 0
    )
    gap_cols = lax.dynamic_slice_in_dim(gaps, first_col, cols_dev, 0)
    pieces = rows_dev // lax.axis_size("col")
    own_rows = lax.dynamic_slice_in_dim(
        cholesky, lax.axis_index("col") * pieces, pieces, 0
    ).astype(F32)
    summed = lax.psum_scatter(
        jnp.dot(amplitudes, chol_cols, preferred_element_type=F32),
        "col",
        scatter_dimension=0,
        tiled=True,
    )
    dressed = (own_rows + summed * pairs**-0.5).astype(BF16)
    w_rows = lax.all_gather(dressed, "col", axis=0, tiled=True)
    w_cols = spread(
        lax.dynamic_slice_in_dim(w_rows, offset, cols_dev, 0), "row", root_row
    )
    product = lax.dot_general(
        w_rows, w_cols, (((1,), (1,)), ((), ())), preferred_element_type=F32
    )
    return (
        -(product * vectors**-0.5) / (gap_rows[:, None] + gap_cols[None, :])
    ).astype(BF16)


def params():
    return pltpu.CompilerParams(vmem_limit_bytes=VMEM_LIMIT)


def cost(flops, nbytes):
    return pl.CostEstimate(flops=flops, bytes_accessed=nbytes, transcendentals=0)


def partial_kernel(where_ref, a0_ref, a1_ref, *refs):
    lows, highs = refs[:4], refs[4:8]
    own_ref, oth_ref, c_ref, sems = refs[-4:]
    part = c_ref.shape[0] // 2

    @pl.when(pl.program_id(0) == 0)
    def _():
        for corner in range(4):

            @pl.when(where_ref[1] == corner)
            def _():
                low = pltpu.make_async_copy(lows[corner], c_ref.at[pl.ds(0, part)], sems.at[0])
                high = pltpu.make_async_copy(highs[corner], c_ref.at[pl.ds(part, part)], sems.at[1])
                low.start()
                high.start()
                low.wait()
                high.wait()

    own_ref[...] = jnp.dot(a0_ref[...], c_ref[...], preferred_element_type=F32)
    oth_ref[...] = jnp.dot(
        a1_ref[...], c_ref[...], preferred_element_type=F32
    ).astype(BF16)


TOKEN = jax.ShapeDtypeStruct((8, 128), F32)


def partial_sums(place, tile, lows, highs, start, size, after):
    rows, depth = tile.shape
    width = lows[0].shape[1]
    half = rows // 2
    step = size // 2
    first, per_half = start // step, half // step
    return pl.pallas_call(
        partial_kernel,
        grid_spec=pltpu.PrefetchScalarGridSpec(
            num_scalar_prefetch=1,
            grid=(size // step,),
            in_specs=[
                pl.BlockSpec((step, depth), lambda i, k: (k[0] * per_half + first + i, 0)),
                pl.BlockSpec((step, depth), lambda i, k: ((1 - k[0]) * per_half + first + i, 0)),
            ]
            + [pl.BlockSpec(memory_space=pl.ANY)] * (8 + len(after)),
            out_specs=[
                pl.BlockSpec((step, width), lambda i, k: (i, 0)),
                pl.BlockSpec((step, width), lambda i, k: (i, 0)),
            ],
            scratch_shapes=[
                pltpu.VMEM((depth, width), BF16),
                pltpu.SemaphoreType.DMA((2,)),
            ],
        ),
        out_shape=[
            jax.ShapeDtypeStruct((size, width), F32),
            jax.ShapeDtypeStruct((size, width), BF16),
        ],
        compiler_params=params(),
        cost_estimate=cost(4 * size * depth * width, 4 * size * (depth + 3 * width)),
        name="partial_sums",
    )(place, tile, tile, *lows, *highs, *after)


def block_out(rows, cols, gap_rows, gap_cols):
    product = lax.dot_general(
        rows, cols, (((1,), (1,)), ((), ())), preferred_element_type=F32
    )
    wide = jnp.concatenate([gap_rows] * (product.shape[1] // gap_rows.shape[1]), axis=1)
    return (product / (wide + gap_cols)).astype(BF16)


def new_rows_kernel(k_ref, own_ref, oth_ref, cols_ref, gr_ref, gc_ref, *refs):
    out_ref, wr_ref, token_ref = refs[-3:]
    token_ref[...] = jnp.zeros_like(token_ref)
    piece = own_ref.shape[0]
    wr_ref[...] = jnp.where(pl.program_id(0) == 0, own_ref[...], oth_ref[...])
    for first in range(0, cols_ref.shape[0], piece):
        here = slice(first, first + piece)
        out_ref[:, here] = block_out(wr_ref[...], cols_ref[here, :], gr_ref[...], gc_ref[:, here])


def new_rows(core, own, oth, cols, gap_rows, gap_cols, start, width, state, shape, after):
    rows, total_cols = shape
    size, vectors = own.shape
    per_half = rows // 2 // size
    first = start // size

    def row(i, k):
        return lax.rem(k[0] + i, 2) * per_half + first

    return pl.pallas_call(
        new_rows_kernel,
        grid_spec=pltpu.PrefetchScalarGridSpec(
            num_scalar_prefetch=1,
            grid=(2,),
            in_specs=[
                pl.BlockSpec((size, vectors), lambda i, k: (0, 0)),
                pl.BlockSpec((size, vectors), lambda i, k: (0, 0)),
                pl.BlockSpec((width, vectors), lambda i, k: (0, 0)),
                pl.BlockSpec((size, gap_rows.shape[1]), lambda i, k: (row(i, k), 0)),
                pl.BlockSpec((1, width), lambda i, k: (0, 0)),
            ]
            + [pl.BlockSpec(memory_space=pl.ANY)] * (len(state) + len(after)),
            out_specs=[
                pl.BlockSpec((size, width), lambda i, k: (row(i, k), 0)),
                pl.BlockSpec((size, vectors), lambda i, k: (row(i, k), 0)),
                pl.BlockSpec((8, 128), lambda i, k: (0, 0)),
            ],
        ),
        out_shape=[
            jax.ShapeDtypeStruct((rows, total_cols), BF16),
            jax.ShapeDtypeStruct((rows, vectors), BF16),
            TOKEN,
        ],
        input_output_aliases={6: 0, 7: 1} if state else {},
        compiler_params=params(),
        cost_estimate=cost(4 * size * width * vectors, 4 * size * width + 2 * width * vectors),
        name="new_rows",
    )(core, own, oth, cols, gap_rows, gap_cols, *state, *after)


def new_cols_kernel(wr_ref, cols_ref, gr_ref, gc_ref, *refs):
    out_ref, wc_ref, token_ref = refs[-3:]
    token_ref[...] = jnp.zeros_like(token_ref)
    out_ref[...] = block_out(wr_ref[...], cols_ref[...], gr_ref[...], gc_ref[...])
    wc_ref[...] = cols_ref[...]


def new_cols(wr, cols, gap_rows, gap_cols, start, out, wc, after):
    rows, vectors = wr.shape
    size = cols.shape[0]
    half, chunks = rows // 2 // size, start // size + 1
    wide = max(d for d in (1, 2) if chunks % d == 0 and half % d == 0)
    tm = wide * size
    per_half, count = half // wide, chunks // wide

    def row(i):
        return (i // count) * per_half + lax.rem(i, count)

    place = start // size
    more = [] if wc is None else [wc]
    return pl.pallas_call(
        new_cols_kernel,
        grid=(2 * count,),
        in_specs=[
            pl.BlockSpec((tm, vectors), lambda i: (row(i), 0)),
            pl.BlockSpec((size, vectors), lambda i: (0, 0)),
            pl.BlockSpec((tm, gap_rows.shape[1]), lambda i: (row(i), 0)),
            pl.BlockSpec((1, size), lambda i: (0, place)),
        ]
        + [pl.BlockSpec(memory_space=pl.ANY)] * (1 + len(more) + len(after)),
        out_specs=[
            pl.BlockSpec((tm, size), lambda i: (row(i), place)),
            pl.BlockSpec((size, vectors), lambda i: (place, 0)),
            pl.BlockSpec((8, 128), lambda i: (0, 0)),
        ],
        out_shape=[
            jax.ShapeDtypeStruct(out.shape, BF16),
            jax.ShapeDtypeStruct((out.shape[1], vectors), BF16),
            TOKEN,
        ],
        input_output_aliases={4: 0, 5: 1} if more else {4: 0},
        compiler_params=params(),
        cost_estimate=cost(4 * (start + size) * size * vectors, 8 * (start + size) * (size + vectors)),
        name="new_cols",
    )(wr, cols, gap_rows, gap_cols, out, *more, *after)


def last_cols_kernel(wr_ref, c0_ref, c1_ref, gr_ref, gc_ref, *refs):
    out_ref = refs[-1]
    size = c0_ref.shape[0]
    for i, c_ref in enumerate((c0_ref, c1_ref)):
        here = slice(i * size, (i + 1) * size)
        out_ref[:, here] = block_out(wr_ref[...], c_ref[...], gr_ref[...], gc_ref[:, here])


def last_cols(wr, cols, gap_rows, gap_cols, start, out, after):
    rows, vectors = wr.shape
    size = cols[0].shape[0]
    place = start // (2 * size)
    return pl.pallas_call(
        last_cols_kernel,
        grid=(rows // size,),
        in_specs=[
            pl.BlockSpec((size, vectors), lambda i: (i, 0)),
            pl.BlockSpec((size, vectors), lambda i: (0, 0)),
            pl.BlockSpec((size, vectors), lambda i: (0, 0)),
            pl.BlockSpec((size, gap_rows.shape[1]), lambda i: (i, 0)),
            pl.BlockSpec((1, 2 * size), lambda i: (0, place)),
        ]
        + [pl.BlockSpec(memory_space=pl.ANY)] * (1 + len(after)),
        out_specs=pl.BlockSpec((size, 2 * size), lambda i: (i, place)),
        out_shape=jax.ShapeDtypeStruct(out.shape, BF16),
        input_output_aliases={5: 0},
        compiler_params=params(),
        cost_estimate=cost(4 * rows * size * vectors, 4 * rows * size),
        name="last_cols",
    )(wr, *cols, gap_rows, gap_cols, out, *after)


def planned_shards(amplitudes, cholesky, gaps):
    rows_dev, cols_dev = amplitudes.shape
    pairs, vectors = gaps.shape[0], cholesky.shape[1]
    n_col = lax.axis_size("col")
    planes = n_col // 2
    row, col = lax.axis_index("row"), lax.axis_index("col")
    plane, core = col // 2, col % 2
    core_arg = core.astype(jnp.int32).reshape(1)
    half = rows_dev // 2

    def in_plane(*hops):
        pairs_list = [
            ((plane_ ^ source) * n_col + 2 * plane_ + core_, (plane_ ^ target) * n_col + 2 * plane_ + core_)
            for source, target in hops
            for plane_ in range(planes)
            for core_ in range(2)
        ]
        return lambda value: lax.ppermute(value, ("row", "col"), pairs_list)

    def in_line(*hops):
        pairs_list = [(2 * a + core_, 2 * b + core_) for a, b in hops for core_ in range(2)]
        return lambda value: lax.ppermute(value, "col", pairs_list)

    root_x, root_y = in_plane((0, 1)), in_plane((0, 2))
    x_far, y_far = in_plane((1, 3)), in_plane((2, 3))
    outer = in_line((0, 1), (1, 0), (2, 3), (3, 2))
    middle = in_line((1, 2), (2, 1))
    swap = lambda value: lax.ppermute(value, "col", [(i, i ^ 1) for i in range(n_col)])
    is_root = row == plane
    in_middle = (plane == 1) | (plane == 2)

    scale = pairs**-0.5
    gap_scale = -(vectors**0.5)
    gap_rows = lax.dynamic_slice_in_dim(gaps, row * rows_dev, rows_dev, 0) * gap_scale
    gap_rows = jnp.broadcast_to(gap_rows[:, None], (rows_dev, 128))
    gap_cols = (lax.dynamic_slice_in_dim(gaps, col * cols_dev, cols_dev, 0) * gap_scale)[None, :]

    part = cols_dev // 2
    low = lax.dynamic_slice_in_dim(cholesky, core * cols_dev, part, 0)
    high = lax.dynamic_slice_in_dim(cholesky, core * cols_dev + part, part, 0)
    low_x, high_y = root_x(low), root_y(high)
    high_x, low_y = root_x(high), root_y(low)
    low_x, gap_rows, gap_cols = lax.optimization_barrier((low_x, gap_rows, gap_cols))
    lows = [low, low_x, low_y, x_far(low_x)]
    highs = [high, high_x, high_y, y_far(high_y)]
    place_arg = jnp.stack([core, row ^ plane]).astype(jnp.int32)

    count = CHUNKS
    size = half // count

    def sums(i, after):
        return partial_sums(place_arg, amplitudes, lows, highs, i * size, size, after)

    def rows(c, known, after, state):
        return new_rows(
            core_arg, final[c], across[c], known, gap_rows, gap_cols,
            c * size, size * min(max(c, 1), count - 2), state, amplitudes.shape, after,
        )

    none = [None] * (count + 4)
    own, mine, dressed, final, cols = (list(none) for _ in range(5))
    sent, other, across, from_x, from_y, from_e, from_m, passed, token = ({} for _ in range(9))
    own[0], first = sums(0, [])
    other[0] = swap(first)
    out = wr = wc = None
    for t in range(count + 3):
        moved, sends = [], []

        def keep(place, key, value):
            place[key] = value
            moved.append((place, key))

        def move(place, key, transfer, value):
            keep(place, key, transfer(value))
            sends.append(value)

        send = None
        if 0 <= t - 2 < count:
            c = t - 2
            chol = lax.dynamic_slice_in_dim(cholesky, core * half + c * size, size, 0)
            total = mine[c].astype(F32) + from_e[c].astype(F32) + from_m[c].astype(F32)
            dressed[c] = send = (chol.astype(F32) + total * scale).astype(BF16)
        if t < count:
            if t == 1:
                other[1] = swap(sent[1])
            mine[t] = (own[t] + other[t].astype(F32)).astype(BF16)
            send = mine[t] if send is None else jnp.where(in_middle, send, mine[t])
        both = None
        if 0 <= t - 1 < count:
            both = (mine[t - 1].astype(F32) + from_e[t - 1].astype(F32)).astype(BF16)
        arrived = from_e.get(t - 1)
        if both is not None and send is not None and t >= 3:
            send, both, arrived = lax.optimization_barrier((send, both, arrived))
        elif send is not None and t >= 3:
            send, arrived = lax.optimization_barrier((send, arrived))
        if send is not None:
            move(from_e, t, outer, send)
        if both is not None:
            move(from_m, t - 1, middle, both)
        c = t - 3
        if 0 <= c < count:
            final[c] = jnp.where(in_middle, dressed[c], arrived)
            move(across, c, swap, final[c])
            if c < count - 1:
                move(from_x, c, root_x, final[c])
                move(from_y, c, root_y, final[c])
            else:
                low_x, high_y = root_x(final[c][: size // 2]), root_y(final[c][size // 2 :])
        if 0 <= t - 4 < count - 2:
            move(passed, t - 4, x_far, from_x[t - 4])
        if 1 <= t < count - 1:
            keep(other, t + 1, swap(sent[t + 1]))
        for i in (1, 2) if t == 0 else (t + 2,):
            if i < count:
                own[i], first = sums(i, sends)
                keep(sent, i, first)
        if t >= 5:
            c = t - 5
            cols[c] = jnp.where(is_root, final[c], from_x[c] + from_y[c] + passed[c])
            before = [*sends, *token.values()]
            if c == 0:
                out, wr, _ = rows(0, cols[0], before, [])
            out, wc, last = new_cols(wr, cols[c], gap_rows, gap_cols, c * size, out, wc, before)
            if t < count + 2:
                out, wr, last = rows(c + 1, wc, before, [out, wr])
                keep(token, 0, last)
        if t < count + 2:
            held = lax.optimization_barrier(tuple(place[key] for place, key in moved))
            for (place, key), value in zip(moved, held):
                place[key] = value
    c = count - 1
    low_far, high_far = x_far(from_x[c - 1][: size // 2]), y_far(from_y[c - 1][size // 2 :])
    low_x, high_y, low_far, high_far, final[c], across[c], last = lax.optimization_barrier(
        (low_x, high_y, low_far, high_far, final[c], across[c], last)
    )
    passed[c - 1] = jnp.concatenate([low_far, high_far], axis=0)
    low, high = final[c][: size // 2], final[c][size // 2 :]
    high_x, low_y = root_x(high), root_y(low)
    low_far, high_far = x_far(low_x), y_far(high_y)
    out, wr, _ = rows(c - 1, wc, [last, low_x, high_y], [out, wr])
    out, wr, last = rows(c, wc, [], [out, wr])
    high_x, low_y, low_far, high_far, last = lax.optimization_barrier(
        (high_x, low_y, low_far, high_far, last)
    )
    cols[c] = jnp.concatenate(
        [
            jnp.where(is_root, low, low_x + low_y + low_far),
            jnp.where(is_root, high, high_x + high_y + high_far),
        ],
        axis=0,
    )
    c = count - 2
    cols[c] = jnp.where(is_root, final[c], from_x[c] + from_y[c] + passed[c])
    return last_cols(wr, cols[c : c + 2], gap_rows, gap_cols, c * size, out, [last])


def solution(mesh):
    in_specs = (P("row", "col"), P("row", None), P())
    out_specs = P("row", "col")
    fits = (mesh.shape["row"], mesh.shape["col"]) == (4, 8)
    shards = planned_shards if fits else general_shards
    return jax.shard_map(
        shards, mesh=mesh, in_specs=in_specs, out_specs=out_specs, check_vma=False
    )
```

```python
import functools

import jax
import jax.numpy as jnp
from jax import lax
from jax.experimental import pallas as pl
from jax.experimental.pallas import tpu as pltpu
from jax.sharding import PartitionSpec as P

BF16, F32 = jnp.bfloat16, jnp.float32
VMEM_LIMIT = 20 * 1024 * 1024
CHUNKS = 4


def spread(value, axis, source):
    kept = jnp.where(lax.axis_index(axis) == source, value, 0).astype(value.dtype)
    return lax.psum(kept, axis)


def general_shards(amplitudes, cholesky, gaps):
    rows_dev, cols_dev = amplitudes.shape
    pairs, vectors = gaps.shape[0], cholesky.shape[1]
    first_col = lax.axis_index("col") * cols_dev
    root_row = first_col // rows_dev
    offset = first_col - root_row * rows_dev
    chol_cols = spread(
        lax.dynamic_slice_in_dim(cholesky, offset, cols_dev, 0), "row", root_row
    )
    gap_rows = lax.dynamic_slice_in_dim(
        gaps, lax.axis_index("row") * rows_dev, rows_dev, 0
    )
    gap_cols = lax.dynamic_slice_in_dim(gaps, first_col, cols_dev, 0)
    pieces = rows_dev // lax.axis_size("col")
    own_rows = lax.dynamic_slice_in_dim(
        cholesky, lax.axis_index("col") * pieces, pieces, 0
    ).astype(F32)
    summed = lax.psum_scatter(
        jnp.dot(amplitudes, chol_cols, preferred_element_type=F32),
        "col",
        scatter_dimension=0,
        tiled=True,
    )
    dressed = (own_rows + summed * pairs**-0.5).astype(BF16)
    w_rows = lax.all_gather(dressed, "col", axis=0, tiled=True)
    w_cols = spread(
        lax.dynamic_slice_in_dim(w_rows, offset, cols_dev, 0), "row", root_row
    )
    product = lax.dot_general(
        w_rows, w_cols, (((1,), (1,)), ((), ())), preferred_element_type=F32
    )
    return (
        -(product * vectors**-0.5) / (gap_rows[:, None] + gap_cols[None, :])
    ).astype(BF16)


def params():
    return pltpu.CompilerParams(vmem_limit_bytes=VMEM_LIMIT)


def cost(flops, nbytes):
    return pl.CostEstimate(flops=flops, bytes_accessed=nbytes, transcendentals=0)


def partial_kernel(where_ref, a0_ref, a1_ref, *refs):
    lows, highs = refs[:4], refs[4:8]
    own_ref, oth_ref, c_ref, sems = refs[-4:]
    part = c_ref.shape[0] // 2

    @pl.when(pl.program_id(0) == 0)
    def _():
        for corner in range(4):

            @pl.when(where_ref[1] == corner)
            def _():
                low = pltpu.make_async_copy(lows[corner], c_ref.at[pl.ds(0, part)], sems.at[0])
                high = pltpu.make_async_copy(highs[corner], c_ref.at[pl.ds(part, part)], sems.at[1])
                low.start()
                high.start()
                low.wait()
                high.wait()

    own_ref[...] = jnp.dot(a0_ref[...], c_ref[...], preferred_element_type=F32)
    oth_ref[...] = jnp.dot(
        a1_ref[...], c_ref[...], preferred_element_type=F32
    ).astype(BF16)


TOKEN = jax.ShapeDtypeStruct((8, 128), F32)


def partial_sums(place, tile, lows, highs, start, size, after):
    rows, depth = tile.shape
    width = lows[0].shape[1]
    half = rows // 2
    step = size // 2
    first, per_half = start // step, half // step
    return pl.pallas_call(
        partial_kernel,
        grid_spec=pltpu.PrefetchScalarGridSpec(
            num_scalar_prefetch=1,
            grid=(size // step,),
            in_specs=[
                pl.BlockSpec((step, depth), lambda i, k: (k[0] * per_half + first + i, 0)),
                pl.BlockSpec((step, depth), lambda i, k: ((1 - k[0]) * per_half + first + i, 0)),
            ]
            + [pl.BlockSpec(memory_space=pl.ANY)] * (8 + len(after)),
            out_specs=[
                pl.BlockSpec((step, width), lambda i, k: (i, 0)),
                pl.BlockSpec((step, width), lambda i, k: (i, 0)),
            ],
            scratch_shapes=[
                pltpu.VMEM((depth, width), BF16),
                pltpu.SemaphoreType.DMA((2,)),
            ],
        ),
        out_shape=[
            jax.ShapeDtypeStruct((size, width), F32),
            jax.ShapeDtypeStruct((size, width), BF16),
        ],
        compiler_params=params(),
        cost_estimate=cost(4 * size * depth * width, 4 * size * (depth + 3 * width)),
        name="partial_sums",
    )(place, tile, tile, *lows, *highs, *after)


def block_out(rows, cols, gap_rows, gap_cols):
    product = lax.dot_general(
        rows, cols, (((1,), (1,)), ((), ())), preferred_element_type=F32
    )
    wide = jnp.concatenate([gap_rows] * (product.shape[1] // gap_rows.shape[1]), axis=1)
    return (product / (wide + gap_cols)).astype(BF16)


def new_rows_kernel(k_ref, own_ref, oth_ref, cols_ref, gr_ref, gc_ref, *refs):
    out_ref, wr_ref, token_ref = refs[-3:]
    token_ref[...] = jnp.zeros_like(token_ref)
    piece = own_ref.shape[0]
    wr_ref[...] = jnp.where(pl.program_id(0) == 0, own_ref[...], oth_ref[...])
    for first in range(0, cols_ref.shape[0], piece):
        here = slice(first, first + piece)
        out_ref[:, here] = block_out(wr_ref[...], cols_ref[here, :], gr_ref[...], gc_ref[:, here])


def new_rows(core, own, oth, cols, gap_rows, gap_cols, start, width, state, shape, after):
    rows, total_cols = shape
    size, vectors = own.shape
    per_half = rows // 2 // size
    first = start // size

    def row(i, k):
        return lax.rem(k[0] + i, 2) * per_half + first

    return pl.pallas_call(
        new_rows_kernel,
        grid_spec=pltpu.PrefetchScalarGridSpec(
            num_scalar_prefetch=1,
            grid=(2,),
            in_specs=[
                pl.BlockSpec((size, vectors), lambda i, k: (0, 0)),
                pl.BlockSpec((size, vectors), lambda i, k: (0, 0)),
                pl.BlockSpec((width, vectors), lambda i, k: (0, 0)),
                pl.BlockSpec((size, gap_rows.shape[1]), lambda i, k: (row(i, k), 0)),
                pl.BlockSpec((1, width), lambda i, k: (0, 0)),
            ]
            + [pl.BlockSpec(memory_space=pl.ANY)] * (len(state) + len(after)),
            out_specs=[
                pl.BlockSpec((size, width), lambda i, k: (row(i, k), 0)),
                pl.BlockSpec((size, vectors), lambda i, k: (row(i, k), 0)),
                pl.BlockSpec((8, 128), lambda i, k: (0, 0)),
            ],
        ),
        out_shape=[
            jax.ShapeDtypeStruct((rows, total_cols), BF16),
            jax.ShapeDtypeStruct((rows, vectors), BF16),
            TOKEN,
        ],
        input_output_aliases={6: 0, 7: 1} if state else {},
        compiler_params=params(),
        cost_estimate=cost(4 * size * width * vectors, 4 * size * width + 2 * width * vectors),
        name="new_rows",
    )(core, own, oth, cols, gap_rows, gap_cols, *state, *after)


def last_rows_kernel(k_ref, own0_ref, oth0_ref, own1_ref, oth1_ref, cols_ref, gr_ref, gc_ref, *refs):
    out_ref, wr_ref, token_ref = refs[-3:]
    token_ref[...] = jnp.zeros_like(token_ref)
    step = pl.program_id(0)
    for i, source in enumerate((own0_ref, own1_ref, oth0_ref, oth1_ref)):

        @pl.when(step == i)
        def _():
            wr_ref[...] = source[...]

    piece = wr_ref.shape[0]
    for first in range(0, cols_ref.shape[0], piece):
        here = slice(first, first + piece)
        out_ref[:, here] = block_out(wr_ref[...], cols_ref[here, :], gr_ref[...], gc_ref[:, here])


def last_rows(core, pieces, cols, gap_rows, gap_cols, start, width, state, after):
    out, wr = state
    size, vectors = pieces[0].shape
    per_half = wr.shape[0] // 2 // size
    first = start // size

    def row(i, k):
        return lax.rem(k[0] + i // 2, 2) * per_half + first + lax.rem(i, 2)

    return pl.pallas_call(
        last_rows_kernel,
        grid_spec=pltpu.PrefetchScalarGridSpec(
            num_scalar_prefetch=1,
            grid=(4,),
            in_specs=[pl.BlockSpec((size, vectors), lambda i, k: (0, 0))] * 4
            + [
                pl.BlockSpec((width, vectors), lambda i, k: (0, 0)),
                pl.BlockSpec((size, gap_rows.shape[1]), lambda i, k: (row(i, k), 0)),
                pl.BlockSpec((1, width), lambda i, k: (0, 0)),
            ]
            + [pl.BlockSpec(memory_space=pl.ANY)] * (2 + len(after)),
            out_specs=[
                pl.BlockSpec((size, width), lambda i, k: (row(i, k), 0)),
                pl.BlockSpec((size, vectors), lambda i, k: (row(i, k), 0)),
                pl.BlockSpec((8, 128), lambda i, k: (0, 0)),
            ],
        ),
        out_shape=[
            jax.ShapeDtypeStruct(out.shape, BF16),
            jax.ShapeDtypeStruct(wr.shape, BF16),
            TOKEN,
        ],
        input_output_aliases={8: 0, 9: 1},
        compiler_params=params(),
        cost_estimate=cost(8 * size * width * vectors, 8 * size * width + 2 * width * vectors),
        name="last_rows",
    )(core, *pieces, cols, gap_rows, gap_cols, out, wr, *after)


def new_cols_kernel(wr_ref, cols_ref, gr_ref, gc_ref, *refs):
    out_ref, wc_ref, token_ref = refs[-3:]
    token_ref[...] = jnp.zeros_like(token_ref)
    out_ref[...] = block_out(wr_ref[...], cols_ref[...], gr_ref[...], gc_ref[...])
    wc_ref[...] = cols_ref[...]


def new_cols(wr, cols, gap_rows, gap_cols, start, out, wc, after):
    rows, vectors = wr.shape
    size = cols.shape[0]
    half, chunks = rows // 2 // size, start // size + 1
    wide = max(d for d in (1, 2) if chunks % d == 0 and half % d == 0)
    tm = wide * size
    per_half, count = half // wide, chunks // wide

    def row(i):
        return (i // count) * per_half + lax.rem(i, count)

    place = start // size
    more = [] if wc is None else [wc]
    return pl.pallas_call(
        new_cols_kernel,
        grid=(2 * count,),
        in_specs=[
            pl.BlockSpec((tm, vectors), lambda i: (row(i), 0)),
            pl.BlockSpec((size, vectors), lambda i: (0, 0)),
            pl.BlockSpec((tm, gap_rows.shape[1]), lambda i: (row(i), 0)),
            pl.BlockSpec((1, size), lambda i: (0, place)),
        ]
        + [pl.BlockSpec(memory_space=pl.ANY)] * (1 + len(more) + len(after)),
        out_specs=[
            pl.BlockSpec((tm, size), lambda i: (row(i), place)),
            pl.BlockSpec((size, vectors), lambda i: (place, 0)),
            pl.BlockSpec((8, 128), lambda i: (0, 0)),
        ],
        out_shape=[
            jax.ShapeDtypeStruct(out.shape, BF16),
            jax.ShapeDtypeStruct((out.shape[1], vectors), BF16),
            TOKEN,
        ],
        input_output_aliases={4: 0, 5: 1} if more else {4: 0},
        compiler_params=params(),
        cost_estimate=cost(4 * (start + size) * size * vectors, 8 * (start + size) * (size + vectors)),
        name="new_cols",
    )(wr, cols, gap_rows, gap_cols, out, *more, *after)


def last_cols_kernel(wr_ref, c0_ref, c1_ref, gr_ref, gc_ref, *refs):
    out_ref = refs[-1]
    size = c0_ref.shape[0]
    for i, c_ref in enumerate((c0_ref, c1_ref)):
        here = slice(i * size, (i + 1) * size)
        out_ref[:, here] = block_out(wr_ref[...], c_ref[...], gr_ref[...], gc_ref[:, here])


def last_cols(wr, cols, gap_rows, gap_cols, start, out, after):
    rows, vectors = wr.shape
    size = cols[0].shape[0]
    place = start // (2 * size)
    return pl.pallas_call(
        last_cols_kernel,
        grid=(rows // size,),
        in_specs=[
            pl.BlockSpec((size, vectors), lambda i: (i, 0)),
            pl.BlockSpec((size, vectors), lambda i: (0, 0)),
            pl.BlockSpec((size, vectors), lambda i: (0, 0)),
            pl.BlockSpec((size, gap_rows.shape[1]), lambda i: (i, 0)),
            pl.BlockSpec((1, 2 * size), lambda i: (0, place)),
        ]
        + [pl.BlockSpec(memory_space=pl.ANY)] * (1 + len(after)),
        out_specs=pl.BlockSpec((size, 2 * size), lambda i: (i, place)),
        out_shape=jax.ShapeDtypeStruct(out.shape, BF16),
        input_output_aliases={5: 0},
        compiler_params=params(),
        cost_estimate=cost(4 * rows * size * vectors, 4 * rows * size),
        name="last_cols",
    )(wr, *cols, gap_rows, gap_cols, out, *after)


def planned_shards(amplitudes, cholesky, gaps):
    rows_dev, cols_dev = amplitudes.shape
    pairs, vectors = gaps.shape[0], cholesky.shape[1]
    n_col = lax.axis_size("col")
    planes = n_col // 2
    row, col = lax.axis_index("row"), lax.axis_index("col")
    plane, core = col // 2, col % 2
    core_arg = core.astype(jnp.int32).reshape(1)
    half = rows_dev // 2

    def in_plane(*hops):
        pairs_list = [
            ((plane_ ^ source) * n_col + 2 * plane_ + core_, (plane_ ^ target) * n_col + 2 * plane_ + core_)
            for source, target in hops
            for plane_ in range(planes)
            for core_ in range(2)
        ]
        return lambda value: lax.ppermute(value, ("row", "col"), pairs_list)

    def in_line(*hops):
        pairs_list = [(2 * a + core_, 2 * b + core_) for a, b in hops for core_ in range(2)]
        return lambda value: lax.ppermute(value, "col", pairs_list)

    root_x, root_y = in_plane((0, 1)), in_plane((0, 2))
    x_far, y_far = in_plane((1, 3)), in_plane((2, 3))
    outer = in_line((0, 1), (1, 0), (2, 3), (3, 2))
    middle = in_line((1, 2), (2, 1))
    swap = lambda value: lax.ppermute(value, "col", [(i, i ^ 1) for i in range(n_col)])
    is_root = row == plane
    in_middle = (plane == 1) | (plane == 2)

    scale = pairs**-0.5
    gap_scale = -(vectors**0.5)
    gap_rows = lax.dynamic_slice_in_dim(gaps, row * rows_dev, rows_dev, 0) * gap_scale
    gap_rows = jnp.broadcast_to(gap_rows[:, None], (rows_dev, 128))
    gap_cols = (lax.dynamic_slice_in_dim(gaps, col * cols_dev, cols_dev, 0) * gap_scale)[None, :]

    part = cols_dev // 2
    low = lax.dynamic_slice_in_dim(cholesky, core * cols_dev, part, 0)
    high = lax.dynamic_slice_in_dim(cholesky, core * cols_dev + part, part, 0)
    low_x, high_y = root_x(low), root_y(high)
    high_x, low_y = root_x(high), root_y(low)
    low_x, gap_rows, gap_cols = lax.optimization_barrier((low_x, gap_rows, gap_cols))
    lows = [low, low_x, low_y, x_far(low_x)]
    highs = [high, high_x, high_y, y_far(high_y)]
    place_arg = jnp.stack([core, row ^ plane]).astype(jnp.int32)

    count = CHUNKS
    size = half // count

    def sums(i, after):
        return partial_sums(place_arg, amplitudes, lows, highs, i * size, size, after)

    def rows(c, known, after, state):
        return new_rows(
            core_arg, final[c], across[c], known, gap_rows, gap_cols,
            c * size, size * min(max(c, 1), count - 2), state, amplitudes.shape, after,
        )

    none = [None] * (count + 4)
    own, mine, dressed, final, cols = (list(none) for _ in range(5))
    sent, other, across, from_x, from_y, from_e, from_m, passed, token = ({} for _ in range(9))
    own[0], first = sums(0, [])
    other[0] = swap(first)
    out = wr = wc = None
    for t in range(count + 3):
        moved, sends = [], []

        def keep(place, key, value):
            place[key] = value
            moved.append((place, key))

        def move(place, key, transfer, value):
            keep(place, key, transfer(value))
            sends.append(value)

        send = None
        if 0 <= t - 2 < count:
            c = t - 2
            chol = lax.dynamic_slice_in_dim(cholesky, core * half + c * size, size, 0)
            total = mine[c].astype(F32) + from_e[c].astype(F32) + from_m[c].astype(F32)
            dressed[c] = send = (chol.astype(F32) + total * scale).astype(BF16)
        if t < count:
            if t == 1:
                other[1] = swap(sent[1])
            mine[t] = (own[t] + other[t].astype(F32)).astype(BF16)
            send = mine[t] if send is None else jnp.where(in_middle, send, mine[t])
        both = None
        if 0 <= t - 1 < count:
            both = (mine[t - 1].astype(F32) + from_e[t - 1].astype(F32)).astype(BF16)
        arrived = from_e.get(t - 1)
        if both is not None and send is not None and t >= 3:
            send, both, arrived = lax.optimization_barrier((send, both, arrived))
        elif send is not None and t >= 3:
            send, arrived = lax.optimization_barrier((send, arrived))
        if send is not None:
            move(from_e, t, outer, send)
        if both is not None:
            move(from_m, t - 1, middle, both)
        c = t - 3
        if 0 <= c < count:
            final[c] = jnp.where(in_middle, dressed[c], arrived)
            move(across, c, swap, final[c])
            if c < count - 1:
                move(from_x, c, root_x, final[c])
                move(from_y, c, root_y, final[c])
            else:
                low_x, high_y = root_x(final[c][: size // 2]), root_y(final[c][size // 2 :])
        if 0 <= t - 4 < count - 2:
            move(passed, t - 4, x_far, from_x[t - 4])
        if 1 <= t < count - 1:
            keep(other, t + 1, swap(sent[t + 1]))
        for i in (1, 2) if t == 0 else (t + 2,):
            if i < count:
                own[i], first = sums(i, sends)
                keep(sent, i, first)
        if t >= 5:
            c = t - 5
            cols[c] = jnp.where(is_root, final[c], from_x[c] + from_y[c] + passed[c])
            before = [*sends, *token.values()]
            if c == 0:
                out, wr, _ = rows(0, cols[0], before, [])
            out, wc, last = new_cols(wr, cols[c], gap_rows, gap_cols, c * size, out, wc, before)
            if t < count + 2:
                out, wr, last = rows(c + 1, wc, before, [out, wr])
                keep(token, 0, last)
        if t < count + 2:
            held = lax.optimization_barrier(tuple(place[key] for place, key in moved))
            for (place, key), value in zip(moved, held):
                place[key] = value
    c = count - 1
    low_far, high_far = x_far(from_x[c - 1][: size // 2]), y_far(from_y[c - 1][size // 2 :])
    low_x, high_y, low_far, high_far, final[c], across[c], last = lax.optimization_barrier(
        (low_x, high_y, low_far, high_far, final[c], across[c], last)
    )
    passed[c - 1] = jnp.concatenate([low_far, high_far], axis=0)
    low, high = final[c][: size // 2], final[c][size // 2 :]
    high_x, low_y = root_x(high), root_y(low)
    low_far, high_far = x_far(low_x), y_far(high_y)
    out, wr, last = last_rows(
        core_arg, (final[c - 1], across[c - 1], final[c], across[c]), wc, gap_rows, gap_cols,
        (c - 1) * size, (c - 1) * size, (out, wr), [last, low_x, high_y],
    )
    high_x, low_y, low_far, high_far, last = lax.optimization_barrier(
        (high_x, low_y, low_far, high_far, last)
    )
    cols[c] = jnp.concatenate(
        [
            jnp.where(is_root, low, low_x + low_y + low_far),
            jnp.where(is_root, high, high_x + high_y + high_far),
        ],
        axis=0,
    )
    c = count - 2
    cols[c] = jnp.where(is_root, final[c], from_x[c] + from_y[c] + passed[c])
    return last_cols(wr, cols[c : c + 2], gap_rows, gap_cols, c * size, out, [last])


def solution(mesh):
    in_specs = (P("row", "col"), P("row", None), P())
    out_specs = P("row", "col")
    fits = (mesh.shape["row"], mesh.shape["col"]) == (4, 8)
    shards = planned_shards if fits else general_shards
    return jax.shard_map(
        shards, mesh=mesh, in_specs=in_specs, out_specs=out_specs, check_vma=False
    )
```

```python
import functools

import jax
import jax.numpy as jnp
from jax import lax
from jax.experimental import pallas as pl
from jax.experimental.pallas import tpu as pltpu
from jax.sharding import PartitionSpec as P

BF16, F32 = jnp.bfloat16, jnp.float32
VMEM_LIMIT = 28 * 1024 * 1024
CHUNKS = 6


def spread(value, axis, source):
    kept = jnp.where(lax.axis_index(axis) == source, value, 0).astype(value.dtype)
    return lax.psum(kept, axis)


def general_shards(amplitudes, cholesky, gaps):
    rows_dev, cols_dev = amplitudes.shape
    pairs, vectors = gaps.shape[0], cholesky.shape[1]
    first_col = lax.axis_index("col") * cols_dev
    root_row = first_col // rows_dev
    offset = first_col - root_row * rows_dev
    chol_cols = spread(
        lax.dynamic_slice_in_dim(cholesky, offset, cols_dev, 0), "row", root_row
    )
    gap_rows = lax.dynamic_slice_in_dim(
        gaps, lax.axis_index("row") * rows_dev, rows_dev, 0
    )
    gap_cols = lax.dynamic_slice_in_dim(gaps, first_col, cols_dev, 0)
    pieces = rows_dev // lax.axis_size("col")
    own_rows = lax.dynamic_slice_in_dim(
        cholesky, lax.axis_index("col") * pieces, pieces, 0
    ).astype(F32)
    summed = lax.psum_scatter(
        jnp.dot(amplitudes, chol_cols, preferred_element_type=F32),
        "col",
        scatter_dimension=0,
        tiled=True,
    )
    dressed = (own_rows + summed * pairs**-0.5).astype(BF16)
    w_rows = lax.all_gather(dressed, "col", axis=0, tiled=True)
    w_cols = spread(
        lax.dynamic_slice_in_dim(w_rows, offset, cols_dev, 0), "row", root_row
    )
    product = lax.dot_general(
        w_rows, w_cols, (((1,), (1,)), ((), ())), preferred_element_type=F32
    )
    return (
        -(product * vectors**-0.5) / (gap_rows[:, None] + gap_cols[None, :])
    ).astype(BF16)


def params():
    return pltpu.CompilerParams(vmem_limit_bytes=VMEM_LIMIT)


def cost(flops, nbytes):
    return pl.CostEstimate(flops=flops, bytes_accessed=nbytes, transcendentals=0)


def partial_kernel(where_ref, a0_ref, a1_ref, *refs):
    lows, highs = refs[:4], refs[4:8]
    own_ref, oth_ref, c_ref, sems = refs[-4:]
    part = c_ref.shape[0] // 2

    @pl.when(pl.program_id(0) == 0)
    def _():
        for corner in range(4):

            @pl.when(where_ref[1] == corner)
            def _():
                low = pltpu.make_async_copy(lows[corner], c_ref.at[pl.ds(0, part)], sems.at[0])
                high = pltpu.make_async_copy(highs[corner], c_ref.at[pl.ds(part, part)], sems.at[1])
                low.start()
                high.start()
                low.wait()
                high.wait()

    own_ref[...] = jnp.dot(a0_ref[...], c_ref[...], preferred_element_type=F32)
    oth_ref[...] = jnp.dot(
        a1_ref[...], c_ref[...], preferred_element_type=F32
    ).astype(BF16)


TOKEN = jax.ShapeDtypeStruct((8, 128), F32)


def partial_sums(place, tile, lows, highs, start, size, after):
    rows, depth = tile.shape
    width = lows[0].shape[1]
    half = rows // 2
    step = size // 2
    first, per_half = start // step, half // step
    return pl.pallas_call(
        partial_kernel,
        grid_spec=pltpu.PrefetchScalarGridSpec(
            num_scalar_prefetch=1,
            grid=(size // step,),
            in_specs=[
                pl.BlockSpec((step, depth), lambda i, k: (k[0] * per_half + first + i, 0)),
                pl.BlockSpec((step, depth), lambda i, k: ((1 - k[0]) * per_half + first + i, 0)),
            ]
            + [pl.BlockSpec(memory_space=pl.ANY)] * (8 + len(after)),
            out_specs=[
                pl.BlockSpec((step, width), lambda i, k: (i, 0)),
                pl.BlockSpec((step, width), lambda i, k: (i, 0)),
            ],
            scratch_shapes=[
                pltpu.VMEM((depth, width), BF16),
                pltpu.SemaphoreType.DMA((2,)),
            ],
        ),
        out_shape=[
            jax.ShapeDtypeStruct((size, width), F32),
            jax.ShapeDtypeStruct((size, width), BF16),
        ],
        compiler_params=params(),
        cost_estimate=cost(4 * size * depth * width, 4 * size * (depth + 3 * width)),
        name="partial_sums",
    )(place, tile, tile, *lows, *highs, *after)


def block_out(rows, cols, gap_rows, gap_cols):
    product = lax.dot_general(
        rows, cols, (((1,), (1,)), ((), ())), preferred_element_type=F32
    )
    wide = jnp.concatenate([gap_rows] * (product.shape[1] // gap_rows.shape[1]), axis=1)
    return (product / (wide + gap_cols)).astype(BF16)


def new_rows_kernel(k_ref, own_ref, oth_ref, cols_ref, gr_ref, gc_ref, *refs):
    out_ref, wr_ref, token_ref = refs[-3:]
    token_ref[...] = jnp.zeros_like(token_ref)
    piece = own_ref.shape[0]
    wr_ref[...] = jnp.where(pl.program_id(0) == 0, own_ref[...], oth_ref[...])
    for first in range(0, cols_ref.shape[0], piece):
        here = slice(first, first + piece)
        out_ref[:, here] = block_out(wr_ref[...], cols_ref[here, :], gr_ref[...], gc_ref[:, here])


def new_rows(core, own, oth, cols, gap_rows, gap_cols, start, width, state, shape, after):
    rows, total_cols = shape
    size, vectors = own.shape
    per_half = rows // 2 // size
    first = start // size

    def row(i, k):
        return lax.rem(k[0] + i, 2) * per_half + first

    return pl.pallas_call(
        new_rows_kernel,
        grid_spec=pltpu.PrefetchScalarGridSpec(
            num_scalar_prefetch=1,
            grid=(2,),
            in_specs=[
                pl.BlockSpec((size, vectors), lambda i, k: (0, 0)),
                pl.BlockSpec((size, vectors), lambda i, k: (0, 0)),
                pl.BlockSpec((width, vectors), lambda i, k: (0, 0)),
                pl.BlockSpec((size, gap_rows.shape[1]), lambda i, k: (row(i, k), 0)),
                pl.BlockSpec((1, width), lambda i, k: (0, 0)),
            ]
            + [pl.BlockSpec(memory_space=pl.ANY)] * (len(state) + len(after)),
            out_specs=[
                pl.BlockSpec((size, width), lambda i, k: (row(i, k), 0)),
                pl.BlockSpec((size, vectors), lambda i, k: (row(i, k), 0)),
                pl.BlockSpec((8, 128), lambda i, k: (0, 0)),
            ],
        ),
        out_shape=[
            jax.ShapeDtypeStruct((rows, total_cols), BF16),
            jax.ShapeDtypeStruct((rows, vectors), BF16),
            TOKEN,
        ],
        input_output_aliases={6: 0, 7: 1} if state else {},
        compiler_params=params(),
        cost_estimate=cost(4 * size * width * vectors, 4 * size * width + 2 * width * vectors),
        name="new_rows",
    )(core, own, oth, cols, gap_rows, gap_cols, *state, *after)


def last_rows_kernel(k_ref, own0_ref, oth0_ref, own1_ref, oth1_ref, cols_ref, gr_ref, gc_ref, *refs):
    out_ref, wr_ref, token_ref = refs[-3:]
    token_ref[...] = jnp.zeros_like(token_ref)
    step = pl.program_id(0)
    for i, source in enumerate((own0_ref, own1_ref, oth0_ref, oth1_ref)):

        @pl.when(step == i)
        def _():
            wr_ref[...] = source[...]

    piece = wr_ref.shape[0]
    for first in range(0, cols_ref.shape[0], piece):
        here = slice(first, first + piece)
        out_ref[:, here] = block_out(wr_ref[...], cols_ref[here, :], gr_ref[...], gc_ref[:, here])


def last_rows(core, pieces, cols, gap_rows, gap_cols, start, width, state, after):
    out, wr = state
    size, vectors = pieces[0].shape
    per_half = wr.shape[0] // 2 // size
    first = start // size

    def row(i, k):
        return lax.rem(k[0] + i // 2, 2) * per_half + first + lax.rem(i, 2)

    return pl.pallas_call(
        last_rows_kernel,
        grid_spec=pltpu.PrefetchScalarGridSpec(
            num_scalar_prefetch=1,
            grid=(4,),
            in_specs=[pl.BlockSpec((size, vectors), lambda i, k: (0, 0))] * 4
            + [
                pl.BlockSpec((width, vectors), lambda i, k: (0, 0)),
                pl.BlockSpec((size, gap_rows.shape[1]), lambda i, k: (row(i, k), 0)),
                pl.BlockSpec((1, width), lambda i, k: (0, 0)),
            ]
            + [pl.BlockSpec(memory_space=pl.ANY)] * (2 + len(after)),
            out_specs=[
                pl.BlockSpec((size, width), lambda i, k: (row(i, k), 0)),
                pl.BlockSpec((size, vectors), lambda i, k: (row(i, k), 0)),
                pl.BlockSpec((8, 128), lambda i, k: (0, 0)),
            ],
        ),
        out_shape=[
            jax.ShapeDtypeStruct(out.shape, BF16),
            jax.ShapeDtypeStruct(wr.shape, BF16),
            TOKEN,
        ],
        input_output_aliases={8: 0, 9: 1},
        compiler_params=params(),
        cost_estimate=cost(8 * size * width * vectors, 8 * size * width + 2 * width * vectors),
        name="last_rows",
    )(core, *pieces, cols, gap_rows, gap_cols, out, wr, *after)


def new_cols_kernel(wr_ref, cols_ref, gr_ref, gc_ref, *refs):
    out_ref, wc_ref, token_ref = refs[-3:]
    token_ref[...] = jnp.zeros_like(token_ref)
    out_ref[...] = block_out(wr_ref[...], cols_ref[...], gr_ref[...], gc_ref[...])
    wc_ref[...] = cols_ref[...]


def new_cols(wr, cols, gap_rows, gap_cols, start, out, wc, after):
    rows, vectors = wr.shape
    size = cols.shape[0]
    half, chunks = rows // 2 // size, start // size + 1
    wide = max(d for d in (1, 2) if chunks % d == 0 and half % d == 0)
    tm = wide * size
    per_half, count = half // wide, chunks // wide

    def row(i):
        return (i // count) * per_half + lax.rem(i, count)

    place = start // size
    more = [] if wc is None else [wc]
    return pl.pallas_call(
        new_cols_kernel,
        grid=(2 * count,),
        in_specs=[
            pl.BlockSpec((tm, vectors), lambda i: (row(i), 0)),
            pl.BlockSpec((size, vectors), lambda i: (0, 0)),
            pl.BlockSpec((tm, gap_rows.shape[1]), lambda i: (row(i), 0)),
            pl.BlockSpec((1, size), lambda i: (0, place)),
        ]
        + [pl.BlockSpec(memory_space=pl.ANY)] * (1 + len(more) + len(after)),
        out_specs=[
            pl.BlockSpec((tm, size), lambda i: (row(i), place)),
            pl.BlockSpec((size, vectors), lambda i: (place, 0)),
            pl.BlockSpec((8, 128), lambda i: (0, 0)),
        ],
        out_shape=[
            jax.ShapeDtypeStruct(out.shape, BF16),
            jax.ShapeDtypeStruct((out.shape[1], vectors), BF16),
            TOKEN,
        ],
        input_output_aliases={4: 0, 5: 1} if more else {4: 0},
        compiler_params=params(),
        cost_estimate=cost(4 * (start + size) * size * vectors, 8 * (start + size) * (size + vectors)),
        name="new_cols",
    )(wr, cols, gap_rows, gap_cols, out, *more, *after)


def last_cols_kernel(wr_ref, c0_ref, c1_ref, gr_ref, gc_ref, *refs):
    out_ref = refs[-1]
    size = c0_ref.shape[0]
    for i, c_ref in enumerate((c0_ref, c1_ref)):
        here = slice(i * size, (i + 1) * size)
        out_ref[:, here] = block_out(wr_ref[...], c_ref[...], gr_ref[...], gc_ref[:, here])


def last_cols(wr, cols, gap_rows, gap_cols, start, out, after):
    rows, vectors = wr.shape
    size = cols[0].shape[0]
    place = start // (2 * size)
    return pl.pallas_call(
        last_cols_kernel,
        grid=(rows // size,),
        in_specs=[
            pl.BlockSpec((size, vectors), lambda i: (i, 0)),
            pl.BlockSpec((size, vectors), lambda i: (0, 0)),
            pl.BlockSpec((size, vectors), lambda i: (0, 0)),
            pl.BlockSpec((size, gap_rows.shape[1]), lambda i: (i, 0)),
            pl.BlockSpec((1, 2 * size), lambda i: (0, place)),
        ]
        + [pl.BlockSpec(memory_space=pl.ANY)] * (1 + len(after)),
        out_specs=pl.BlockSpec((size, 2 * size), lambda i: (i, place)),
        out_shape=jax.ShapeDtypeStruct(out.shape, BF16),
        input_output_aliases={5: 0},
        compiler_params=params(),
        cost_estimate=cost(4 * rows * size * vectors, 4 * rows * size),
        name="last_cols",
    )(wr, *cols, gap_rows, gap_cols, out, *after)


def planned_shards(amplitudes, cholesky, gaps):
    rows_dev, cols_dev = amplitudes.shape
    pairs, vectors = gaps.shape[0], cholesky.shape[1]
    n_col = lax.axis_size("col")
    planes = n_col // 2
    row, col = lax.axis_index("row"), lax.axis_index("col")
    plane, core = col // 2, col % 2
    core_arg = core.astype(jnp.int32).reshape(1)
    half = rows_dev // 2

    def in_plane(*hops):
        pairs_list = [
            ((plane_ ^ source) * n_col + 2 * plane_ + core_, (plane_ ^ target) * n_col + 2 * plane_ + core_)
            for source, target in hops
            for plane_ in range(planes)
            for core_ in range(2)
        ]
        return lambda value: lax.ppermute(value, ("row", "col"), pairs_list)

    def in_line(*hops):
        pairs_list = [(2 * a + core_, 2 * b + core_) for a, b in hops for core_ in range(2)]
        return lambda value: lax.ppermute(value, "col", pairs_list)

    root_x, root_y = in_plane((0, 1)), in_plane((0, 2))
    x_far, y_far = in_plane((1, 3)), in_plane((2, 3))
    outer = in_line((0, 1), (1, 0), (2, 3), (3, 2))
    middle = in_line((1, 2), (2, 1))
    swap = lambda value: lax.ppermute(value, "col", [(i, i ^ 1) for i in range(n_col)])
    is_root = row == plane
    in_middle = (plane == 1) | (plane == 2)

    scale = pairs**-0.5
    gap_scale = -(vectors**0.5)
    gap_rows = lax.dynamic_slice_in_dim(gaps, row * rows_dev, rows_dev, 0) * gap_scale
    gap_rows = jnp.broadcast_to(gap_rows[:, None], (rows_dev, 128))
    gap_cols = (lax.dynamic_slice_in_dim(gaps, col * cols_dev, cols_dev, 0) * gap_scale)[None, :]

    part = cols_dev // 2
    low = lax.dynamic_slice_in_dim(cholesky, core * cols_dev, part, 0)
    high = lax.dynamic_slice_in_dim(cholesky, core * cols_dev + part, part, 0)
    low_x, high_y = root_x(low), root_y(high)
    high_x, low_y = root_x(high), root_y(low)
    low_x, gap_rows, gap_cols = lax.optimization_barrier((low_x, gap_rows, gap_cols))
    lows = [low, low_x, low_y, x_far(low_x)]
    highs = [high, high_x, high_y, y_far(high_y)]
    place_arg = jnp.stack([core, row ^ plane]).astype(jnp.int32)

    count = CHUNKS
    size = half // count

    def sums(i, after):
        return partial_sums(place_arg, amplitudes, lows, highs, i * size, size, after)

    def rows(c, known, after, state):
        return new_rows(
            core_arg, final[c], across[c], known, gap_rows, gap_cols,
            c * size, size * min(max(c, 1), count - 2), state, amplitudes.shape, after,
        )

    none = [None] * (count + 4)
    own, mine, dressed, final, cols = (list(none) for _ in range(5))
    sent, other, across, from_x, from_y, from_e, from_m, passed, token = ({} for _ in range(9))
    own[0], first = sums(0, [])
    other[0] = swap(first)
    out = wr = wc = None
    for t in range(count + 3):
        moved, sends = [], []

        def keep(place, key, value):
            place[key] = value
            moved.append((place, key))

        def move(place, key, transfer, value):
            keep(place, key, transfer(value))
            sends.append(value)

        send = None
        if 0 <= t - 2 < count:
            c = t - 2
            chol = lax.dynamic_slice_in_dim(cholesky, core * half + c * size, size, 0)
            total = mine[c].astype(F32) + from_e[c].astype(F32) + from_m[c].astype(F32)
            dressed[c] = send = (chol.astype(F32) + total * scale).astype(BF16)
        if t < count:
            if t == 1:
                other[1] = swap(sent[1])
            mine[t] = (own[t] + other[t].astype(F32)).astype(BF16)
            send = mine[t] if send is None else jnp.where(in_middle, send, mine[t])
        both = None
        if 0 <= t - 1 < count:
            both = (mine[t - 1].astype(F32) + from_e[t - 1].astype(F32)).astype(BF16)
        arrived = from_e.get(t - 1)
        if both is not None and send is not None and t >= 3:
            send, both, arrived = lax.optimization_barrier((send, both, arrived))
        elif send is not None and t >= 3:
            send, arrived = lax.optimization_barrier((send, arrived))
        if send is not None:
            move(from_e, t, outer, send)
        if both is not None:
            move(from_m, t - 1, middle, both)
        c = t - 3
        if 0 <= c < count:
            final[c] = jnp.where(in_middle, dressed[c], arrived)
            move(across, c, swap, final[c])
            if c < count - 1:
                move(from_x, c, root_x, final[c])
                move(from_y, c, root_y, final[c])
            else:
                low_x, high_y = root_x(final[c][: size // 2]), root_y(final[c][size // 2 :])
        if 0 <= t - 4 < count - 2:
            move(passed, t - 4, x_far, from_x[t - 4])
        if 1 <= t < count - 1:
            keep(other, t + 1, swap(sent[t + 1]))
        for i in (1, 2) if t == 0 else (t + 2,):
            if i < count:
                own[i], first = sums(i, sends)
                keep(sent, i, first)
        if t >= 5:
            c = t - 5
            cols[c] = jnp.where(is_root, final[c], from_x[c] + from_y[c] + passed[c])
            before = [*sends, *token.values()]
            if c == 0:
                out, wr, _ = rows(0, cols[0], before, [])
            out, wc, last = new_cols(wr, cols[c], gap_rows, gap_cols, c * size, out, wc, before)
            if t < count + 2:
                out, wr, last = rows(c + 1, wc, before, [out, wr])
                keep(token, 0, last)
        if t < count + 2:
            held = lax.optimization_barrier(tuple(place[key] for place, key in moved))
            for (place, key), value in zip(moved, held):
                place[key] = value
    c = count - 1
    low_far, high_far = x_far(from_x[c - 1][: size // 2]), y_far(from_y[c - 1][size // 2 :])
    low_x, high_y, low_far, high_far, final[c], across[c], last = lax.optimization_barrier(
        (low_x, high_y, low_far, high_far, final[c], across[c], last)
    )
    passed[c - 1] = jnp.concatenate([low_far, high_far], axis=0)
    low, high = final[c][: size // 2], final[c][size // 2 :]
    high_x, low_y = root_x(high), root_y(low)
    low_far, high_far = x_far(low_x), y_far(high_y)
    out, wr, last = last_rows(
        core_arg, (final[c - 1], across[c - 1], final[c], across[c]), wc, gap_rows, gap_cols,
        (c - 1) * size, (c - 1) * size, (out, wr), [last, low_x, high_y],
    )
    high_x, low_y, low_far, high_far, last = lax.optimization_barrier(
        (high_x, low_y, low_far, high_far, last)
    )
    cols[c] = jnp.concatenate(
        [
            jnp.where(is_root, low, low_x + low_y + low_far),
            jnp.where(is_root, high, high_x + high_y + high_far),
        ],
        axis=0,
    )
    c = count - 2
    cols[c] = jnp.where(is_root, final[c], from_x[c] + from_y[c] + passed[c])
    return last_cols(wr, cols[c : c + 2], gap_rows, gap_cols, c * size, out, [last])


def solution(mesh):
    in_specs = (P("row", "col"), P("row", None), P())
    out_specs = P("row", "col")
    fits = (mesh.shape["row"], mesh.shape["col"]) == (4, 8)
    shards = planned_shards if fits else general_shards
    return jax.shard_map(
        shards, mesh=mesh, in_specs=in_specs, out_specs=out_specs, check_vma=False
    )
```
